32 devices in a mesh: grp: 2 (over core), row: 4 (over z), col: 4 (over y, x).
Axes of the slice: x: 2, y: 2, z: 4, core: 2. Of those that a mesh axis runs over, the one named last changes fastest.
Arguments:
- cost_matrix: float32 [2, 4096, 4096], P('grp', 'row', 'col'), may hold values from -0.125 to 0.125
- coupling_factors: float32 [2, 4096, 1024], P('grp', ('row', 'col')), may hold values from 0.25 to 4
Outputs:
- updated_factors: float32 [2, 4096, 1024], P('grp', ('row', 'col'))
The draws below stay inside these ranges and needn't reach their ends.
All inputs are finite; a program needn't handle non-finite values. Where the reference program divides by a largest or mean magnitude, that divisor is 1e-20 or more.
Results may differ from the reference program's by a relative error of at most 0.0003.
Values sent between devices are 32-bit elements; how exact they have to be, the bound alone decides.
A program may use at most 64 MiB of HBM per device.

```python
import math
import jax
import jax.numpy as jnp
from jax import lax

RANK = 1024
STEPS = 2
N = 4096


def with_spikes(values, stream_key, source, target, parts, factor):
    owner, partner = [(jnp.arange(values.shape[axis_at]) // (values.shape[axis_at] // parts)).reshape([-1 if axis == axis_at else 1 for axis in range(values.ndim)]) for axis_at in (source, target)]
    chosen = jax.random.permutation(stream_key, parts)[partner]
    strong = (owner == chosen) | (owner == (partner + parts // 2) % parts)
    return jnp.where(strong, factor * values, values)


def shard_levels(stream_key, dims, pieces, least, top_value):
    loudness = 1.0
    for position, shards_of in pieces:
        draws = jax.random.uniform(jax.random.fold_in(jax.random.fold_in(stream_key, 6), position), (shards_of,), jnp.float32, least / len(pieces), top_value / len(pieces))
        loudness = loudness * jnp.repeat(jnp.exp(draws), dims[position] // shards_of).reshape((-1,) + (1,) * (len(dims) - 1 - position))
    return loudness


def gaussian_with(stream_key, extent, deviation, limit, split, heavy, kind=jnp.bfloat16):
    result = deviation * jax.random.normal(stream_key, extent, jnp.float32)
    if split:
        result = result * shard_levels(stream_key, extent, split, -0.22, 0.18)
    return jnp.clip(with_spikes(result, jax.random.fold_in(stream_key, 3), *heavy), -limit, limit).astype(kind)


def setup_inputs(seed: int = 0) -> dict:
    streams_of = jax.random.split(jax.random.key(seed), 3)
    cost_matrix = gaussian_with(streams_of[0], (2, N, N), N ** -0.5, 0.125, ((0, 2), (1, 4), (2, 4)), (2, 1, 4, 2.0), jnp.float32)
    coupling_factors = jnp.clip(jnp.exp(math.log(4.0) - 2.7725887 * jax.random.uniform(streams_of[1], (2, N, RANK), jnp.float32) ** shard_levels(streams_of[1], (2, N, RANK), ((0, 2), (1, 16)), -0.2, 0.2)), 0.25, 4.0)
    return {"cost_matrix": cost_matrix, "coupling_factors": coupling_factors}


def reference(cost_matrix, coupling_factors):
    rank_width = coupling_factors.shape[2]
    factor_list = [coupling_factors[0], coupling_factors[1]]
    for iteration in range(STEPS):
        mixed = [jnp.dot(cost_matrix[group_id], factor_list[group_id], precision=lax.Precision.HIGHEST, preferred_element_type=jnp.float32) for group_id in range(2)]
        cores = [jnp.dot(factor_list[group_id].T, mixed[group_id], precision=lax.Precision.HIGHEST, preferred_element_type=jnp.float32) for group_id in range(2)]
        updated = []
        for group_id in range(2):
            gradient = jnp.dot(mixed[group_id], cores[1 - group_id], precision=lax.Precision.HIGHEST, preferred_element_type=jnp.float32)
            row_scale = jnp.max(jnp.abs(gradient), axis=1, keepdims=True) + 1e-6
            exponent = -3.0 * gradient / row_scale
            weighted = factor_list[group_id] * jnp.exp(exponent)
            updated.append(rank_width * weighted / jnp.sum(weighted, axis=1, keepdims=True))
        factor_list = updated
    return jnp.stack(factor_list)
```

```python
import functools
import jax
import jax.numpy as jnp
from jax import lax
from jax.experimental import pallas as pl
from jax.experimental.pallas import tpu as pltpu
from jax.sharding import PartitionSpec as P

STEPS = 2
MESH = pl.DeviceIdType.MESH
PARTS = 4
VMEM_BYTES = 48 * 1024 * 1024


def peer(axis, bit):
    index = lax.axis_index(axis)
    mine = (index // 2**bit) % 2
    return mine, index + (1 - 2 * mine) * 2**bit


def rows_at(offset, size):
    if isinstance(offset, int):
        return pl.ds(offset, size)
    return pl.ds(pl.multiple_of(offset, 8), size)


def remote(src, dst, send_sem, recv_sem, device):
    return pltpu.make_async_remote_copy(
        src_ref=src,
        dst_ref=dst,
        send_sem=send_sem,
        recv_sem=recv_sem,
        device_id=device,
        device_id_type=MESH,
    )


def greet(devices):
    barrier = pltpu.get_barrier_semaphore()
    for device in devices:
        pl.semaphore_signal(barrier, inc=1, device_id=device, device_id_type=MESH)
    pl.semaphore_wait(barrier, len(devices))


def gather_kernel(x_ref, panel, held, z_send, z_recv, p_send, p_recv, own_sem):
    n = lax.axis_size("row")
    r = lax.axis_index("row")
    c = lax.axis_index("col")
    size = x_ref.shape[0] // PARTS

    barrier = pltpu.get_barrier_semaphore()
    for step in range(1, n):
        pl.semaphore_signal(
            barrier, inc=1, device_id={"col": lax.rem(c + step, n)}, device_id_type=MESH
        )
    for away in (-1, 1):

        @pl.when((r + away >= 0) & (r + away < n))
        def _():
            pl.semaphore_signal(barrier, inc=1, device_id={"row": r + away}, device_id_type=MESH)

    pl.semaphore_wait(barrier, n - 1 + (r + n - 1) // n + (2 * n - 2 - r) // n)

    def along(src, k, s, way):
        rows = pl.ds(k * size, size)
        return remote(
            src.at[rows], held.at[s, rows], z_send.at[k, s, way], z_recv.at[k, s], {"row": r + 2 * way - 1}
        )

    def across(src, k, s):
        rows = pl.ds(k * size, size)
        return remote(src.at[rows], panel.at[c, rows], p_send.at[k, s], p_recv.at[k, c], {"col": s})

    def keep(src, k):
        rows = pl.ds(k * size, size)
        return pltpu.make_async_copy(src.at[rows], panel.at[c, rows], own_sem.at[k])

    def forward(src, k, s, ways, act):
        for way in ways:
            away = 2 * way - 1

            @pl.when((r + away >= 0) & (r + away < n))
            def _():
                act(along(src, k, s, way), False)

        @pl.when(s != c)
        def _():
            act(across(src, k, s), False)

        @pl.when(s == c)
        def _():
            act(keep(src, k), True)

    def begin(copy, local):
        copy.start()

    def end(copy, local):
        copy.wait() if local else copy.wait_send()

    forward(x_ref, 0, r, (0, 1), begin)
    for k in range(PARTS):
        if k + 1 < PARTS:
            forward(x_ref, k + 1, r, (0, 1), begin)
        for distance in range(1, n):
            for way in (0, 1):
                s = r - (2 * way - 1) * distance

                @pl.when((s >= 0) & (s < n))
                def _():
                    along(held.at[s], k, s, way).wait_recv()
                    forward(held.at[s], k, s, (way,), begin)

    for k in range(PARTS):
        rows = pl.ds(k * size, size)
        forward(x_ref, k, r, (0, 1), end)
        for distance in range(1, n):
            for way in (0, 1):
                s = r - (2 * way - 1) * distance

                @pl.when((s >= 0) & (s < n))
                def _():
                    forward(held.at[s], k, s, (way,), end)

        for step in range(1, n):
            source = lax.rem(c + step, n)
            remote(
                x_ref.at[rows],
                panel.at[source, rows],
                p_send.at[k, source],
                p_recv.at[k, source],
                {"col": source},
            ).wait_recv()


def gathered(current):
    n = lax.axis_size("row")
    rows, width = current.shape
    return pl.pallas_call(
        gather_kernel,
        out_shape=jax.ShapeDtypeStruct((n, rows, width), jnp.float32),
        in_specs=[pl.BlockSpec(memory_space=pltpu.VMEM)],
        out_specs=pl.BlockSpec(memory_space=pltpu.VMEM),
        scratch_shapes=[
            pltpu.VMEM((n, rows, width), jnp.float32),
            pltpu.SemaphoreType.DMA((PARTS, n, 2)),
            pltpu.SemaphoreType.DMA((PARTS, n)),
            pltpu.SemaphoreType.DMA((PARTS, n)),
            pltpu.SemaphoreType.DMA((PARTS, n)),
            pltpu.SemaphoreType.DMA((PARTS,)),
        ],
        compiler_params=pltpu.CompilerParams(
            collective_id=0, has_side_effects=True, vmem_limit_bytes=VMEM_BYTES
        ),
        name="gather",
    )(current)


def scatter_kernel(bits, part, out, acc, recv, send_sem, recv_sem):
    greet([{"col": peer("col", bit)[1]} for bit in range(bits)])
    rows, width = out.shape
    streams = []
    for piece in range(2):
        for order in (list(range(bits)), list(range(bits))[::-1]):
            streams.append((piece, len(streams) % 2, order))

    def spans(q):
        piece, side, _ = streams[q]
        return (pl.ds(piece * (rows // 2), rows // 2), pl.ds(side * (width // 2), width // 2))

    def stage(q, k):
        order = streams[q][2]
        fixed = sum([peer("col", order[j])[0] * 2 ** order[j] for j in range(k)], 0)
        mine, partner = peer("col", order[k])
        free = [0]
        for j in order[k + 1 :]:
            free = free + [f + 2**j for f in free]
        base = sum(2 ** (bits - 1 - j) for j in range(k))
        src = part if k == 0 else acc
        items = []
        for at, f in enumerate(free):
            slot = base + at
            kept = fixed + mine * 2 ** order[k] + f
            sent = fixed + (1 - mine) * 2 ** order[k] + f
            copy = remote(
                src.at[(sent, *spans(q))],
                recv.at[q, slot],
                send_sem.at[q, slot],
                recv_sem.at[q, slot],
                {"col": partner},
            )
            items.append((copy, src, kept, slot))
        return items

    for k in range(bits + 1):
        for q in range(len(streams)):
            if k > 0:
                for copy, src, kept, slot in stage(q, k - 1):
                    copy.wait()
                    total = src[(kept, *spans(q))] + recv[q, slot]
                    if k == bits:
                        out[spans(q)] = total
                    else:
                        acc[(kept, *spans(q))] = total
            if k < bits:
                for copy, _, _, _ in stage(q, k):
                    copy.start()


def scattered(part):
    n = lax.axis_size("col")
    bits = n.bit_length() - 1
    rows, width = part.shape[0] // n, part.shape[1]
    return pl.pallas_call(
        functools.partial(scatter_kernel, bits),
        out_shape=jax.ShapeDtypeStruct((rows, width), jnp.float32),
        in_specs=[pl.BlockSpec(memory_space=pltpu.VMEM)],
        out_specs=pl.BlockSpec(memory_space=pltpu.VMEM),
        scratch_shapes=[
            pltpu.VMEM((n, rows, width), jnp.float32),
            pltpu.VMEM((4, n - 1, rows // 2, width // 2), jnp.float32),
            pltpu.SemaphoreType.DMA((4, n - 1)),
            pltpu.SemaphoreType.DMA((4, n - 1)),
        ],
        compiler_params=pltpu.CompilerParams(
            collective_id=1, has_side_effects=True, vmem_limit_bytes=VMEM_BYTES
        ),
        name="scatter",
    )(part.reshape(n, rows, width))


def core_kernel(row_bits, col_bits, part, out, acc, recv, send_sem, recv_sem):
    rows_axis = [("row", bit) for bit in range(row_bits)]
    cols_axis = [("col", bit) for bit in range(col_bits)]
    swap = {"grp": 1 - lax.axis_index("grp")}
    greet([{axis: peer(axis, bit)[1]} for axis, bit in rows_axis + cols_axis] + [swap])
    width = part.shape[0]
    half = width // 2
    orders = [
        cols_axis + rows_axis,
        cols_axis[::-1] + rows_axis,
        rows_axis[:1] + cols_axis + rows_axis[1:],
        rows_axis[:1] + cols_axis[::-1] + rows_axis[1:],
    ]
    depth = row_bits + col_bits
    phases = 2 * depth + 1
    offsets = []
    for q, order in enumerate(orders):
        track = [(q // 2) * half]
        for k, (axis, bit) in enumerate(order):
            track.append(track[-1] + peer(axis, bit)[0] * (half >> (k + 1)))
        offsets.append(track)

    def describe(q, p):
        columns = pl.ds((q % 2) * half, half)
        sems = (send_sem.at[q, p], recv_sem.at[q, p])
        if p < depth:
            axis, bit = orders[q][p]
            mine, partner = peer(axis, bit)
            size = half >> (p + 1)
            sent = rows_at(offsets[q][p] + (1 - mine) * size, size)
            src = part if p == 0 else acc
            slot = pl.ds(half - (half >> p), size)
            return remote(src.at[sent, columns], recv.at[q, slot], *sems, {axis: partner})
        if p == depth:
            rows = rows_at(offsets[q][depth], half >> depth)
            return remote(acc.at[rows, columns], out.at[rows, columns], *sems, swap)
        level = 2 * depth + 1 - p
        axis, bit = orders[q][level - 1]
        rows = rows_at(offsets[q][level], half >> level)
        return remote(
            out.at[rows, columns], out.at[rows, columns], *sems, {axis: peer(axis, bit)[1]}
        )

    def finish(q, p):
        describe(q, p).wait()
        if p < depth:
            columns = pl.ds((q % 2) * half, half)
            size = half >> (p + 1)
            kept = rows_at(offsets[q][p + 1], size)
            src = part if p == 0 else acc
            acc[kept, columns] = src[kept, columns] + recv[q, pl.ds(half - (half >> p), size)]

    for p in range(phases + 1):
        for q in range(len(orders)):
            if p > 0:
                finish(q, p - 1)
            if p < phases:
                describe(q, p).start()


def other_core_of(part):
    width = part.shape[0]
    row_bits = lax.axis_size("row").bit_length() - 1
    col_bits = lax.axis_size("col").bit_length() - 1
    phases = 2 * (row_bits + col_bits) + 1
    return pl.pallas_call(
        functools.partial(core_kernel, row_bits, col_bits),
        out_shape=jax.ShapeDtypeStruct((width, width), jnp.float32),
        in_specs=[pl.BlockSpec(memory_space=pltpu.VMEM)],
        out_specs=pl.BlockSpec(memory_space=pltpu.VMEM),
        scratch_shapes=[
            pltpu.VMEM((width, width), jnp.float32),
            pltpu.VMEM((4, width // 2, width // 2), jnp.float32),
            pltpu.SemaphoreType.DMA((4, phases)),
            pltpu.SemaphoreType.DMA((4, phases)),
        ],
        compiler_params=pltpu.CompilerParams(
            collective_id=2, has_side_effects=True, vmem_limit_bytes=VMEM_BYTES
        ),
        name="core",
    )(part)


def shards(cost_matrix, coupling_factors):
    cost_tile = cost_matrix[0]
    current = coupling_factors[0]
    blk_rows = cost_tile.shape[0]
    rank_width = current.shape[1]
    for iteration in range(STEPS):
        panel_rows = gathered(current).reshape(blk_rows, rank_width)
        mixed = scattered(
            jnp.dot(
                cost_tile,
                panel_rows,
                precision=lax.Precision.HIGH,
                preferred_element_type=jnp.float32,
            )
        )
        core_part = lax.dot_general(
            current,
            mixed,
            (((0,), (0,)), ((), ())),
            precision=lax.Precision.HIGH,
            preferred_element_type=jnp.float32,
        )
        other_core = other_core_of(core_part)
        gradient = jnp.dot(
            mixed, other_core, precision=lax.Precision.HIGH, preferred_element_type=jnp.float32
        )
        row_scale = jnp.max(jnp.abs(gradient), axis=1, keepdims=True) + 1e-06
        exponent = -3.0 * gradient / row_scale
        weighted = current * jnp.exp(exponent)
        current = rank_width * weighted / jnp.sum(weighted, axis=1, keepdims=True)
    return current[None]


def solution(mesh):
    in_specs = (P("grp", "row", "col"), P("grp", ("row", "col"), None))
    out_specs = P("grp", ("row", "col"), None)
    return jax.shard_map(shards, mesh=mesh, in_specs=in_specs, out_specs=out_specs, check_vma=False)
```

```python
import functools
import jax
import jax.numpy as jnp
from jax import lax
from jax.experimental import pallas as pl
from jax.experimental.pallas import tpu as pltpu
from jax.sharding import PartitionSpec as P

STEPS = 2
MESH = pl.DeviceIdType.MESH
PARTS = 8
VMEM_BYTES = 48 * 1024 * 1024


def peer(axis, bit):
    index = lax.axis_index(axis)
    mine = (index // 2**bit) % 2
    return mine, index + (1 - 2 * mine) * 2**bit


def rows_at(offset, size):
    if isinstance(offset, int):
        return pl.ds(offset, size)
    return pl.ds(pl.multiple_of(offset, 8), size)


def remote(src, dst, send_sem, recv_sem, device):
    return pltpu.make_async_remote_copy(
        src_ref=src,
        dst_ref=dst,
        send_sem=send_sem,
        recv_sem=recv_sem,
        device_id=device,
        device_id_type=MESH,
    )


def greet(devices):
    barrier = pltpu.get_barrier_semaphore()
    for device in devices:
        pl.semaphore_signal(barrier, inc=1, device_id=device, device_id_type=MESH)
    pl.semaphore_wait(barrier, len(devices))


def gather_kernel(x_ref, panel, held, z_send, z_recv, p_send, p_recv, own_sem):
    n = lax.axis_size("row")
    r = lax.axis_index("row")
    c = lax.axis_index("col")
    size = x_ref.shape[0] // PARTS

    barrier = pltpu.get_barrier_semaphore()
    for step in range(1, n):
        pl.semaphore_signal(
            barrier, inc=1, device_id={"col": lax.rem(c + step, n)}, device_id_type=MESH
        )
    for away in (-1, 1):

        @pl.when((r + away >= 0) & (r + away < n))
        def _():
            pl.semaphore_signal(barrier, inc=1, device_id={"row": r + away}, device_id_type=MESH)

    pl.semaphore_wait(barrier, n - 1 + (r + n - 1) // n + (2 * n - 2 - r) // n)

    def along(src, k, s, way):
        rows = pl.ds(k * size, size)
        return remote(
            src.at[rows], held.at[s, rows], z_send.at[k, s, way], z_recv.at[k, s], {"row": r + 2 * way - 1}
        )

    def across(src, k, s):
        rows = pl.ds(k * size, size)
        return remote(src.at[rows], panel.at[c, rows], p_send.at[k, s], p_recv.at[k, c], {"col": s})

    def keep(src, k):
        rows = pl.ds(k * size, size)
        return pltpu.make_async_copy(src.at[rows], panel.at[c, rows], own_sem.at[k])

    def forward(src, k, s, ways, act):
        for way in ways:
            away = 2 * way - 1

            @pl.when((r + away >= 0) & (r + away < n))
            def _():
                act(along(src, k, s, way), False)

        @pl.when(s != c)
        def _():
            act(across(src, k, s), False)

        @pl.when(s == c)
        def _():
            act(keep(src, k), True)

    def begin(copy, local):
        copy.start()

    def end(copy, local):
        copy.wait() if local else copy.wait_send()

    forward(x_ref, 0, r, (0, 1), begin)
    for k in range(PARTS):
        if k + 1 < PARTS:
            forward(x_ref, k + 1, r, (0, 1), begin)
        for distance in range(1, n):
            for way in (0, 1):
                s = r - (2 * way - 1) * distance

                @pl.when((s >= 0) & (s < n))
                def _():
                    along(held.at[s], k, s, way).wait_recv()
                    forward(held.at[s], k, s, (way,), begin)

    for k in range(PARTS):
        rows = pl.ds(k * size, size)
        forward(x_ref, k, r, (0, 1), end)
        for distance in range(1, n):
            for way in (0, 1):
                s = r - (2 * way - 1) * distance

                @pl.when((s >= 0) & (s < n))
                def _():
                    forward(held.at[s], k, s, (way,), end)

        for step in range(1, n):
            source = lax.rem(c + step, n)
            remote(
                x_ref.at[rows],
                panel.at[source, rows],
                p_send.at[k, source],
                p_recv.at[k, source],
                {"col": source},
            ).wait_recv()


def gathered(current):
    n = lax.axis_size("row")
    rows, width = current.shape
    return pl.pallas_call(
        gather_kernel,
        out_shape=jax.ShapeDtypeStruct((n, rows, width), jnp.float32),
        in_specs=[pl.BlockSpec(memory_space=pltpu.VMEM)],
        out_specs=pl.BlockSpec(memory_space=pltpu.VMEM),
        scratch_shapes=[
            pltpu.VMEM((n, rows, width), jnp.float32),
            pltpu.SemaphoreType.DMA((PARTS, n, 2)),
            pltpu.SemaphoreType.DMA((PARTS, n)),
            pltpu.SemaphoreType.DMA((PARTS, n)),
            pltpu.SemaphoreType.DMA((PARTS, n)),
            pltpu.SemaphoreType.DMA((PARTS,)),
        ],
        compiler_params=pltpu.CompilerParams(
            collective_id=0, has_side_effects=True, vmem_limit_bytes=VMEM_BYTES
        ),
        name="gather",
    )(current)


def scatter_kernel(bits, part, out, acc, recv, send_sem, recv_sem):
    greet([{"col": peer("col", bit)[1]} for bit in range(bits)])
    rows, width = out.shape
    streams = []
    for piece in range(2):
        for order in (list(range(bits)), list(range(bits))[::-1]):
            streams.append((piece, len(streams) % 2, order))

    def spans(q):
        piece, side, _ = streams[q]
        return (pl.ds(piece * (rows // 2), rows // 2), pl.ds(side * (width // 2), width // 2))

    def stage(q, k):
        order = streams[q][2]
        fixed = sum([peer("col", order[j])[0] * 2 ** order[j] for j in range(k)], 0)
        mine, partner = peer("col", order[k])
        free = [0]
        for j in order[k + 1 :]:
            free = free + [f + 2**j for f in free]
        base = sum(2 ** (bits - 1 - j) for j in range(k))
        src = part if k == 0 else acc
        items = []
        for at, f in enumerate(free):
            slot = base + at
            kept = fixed + mine * 2 ** order[k] + f
            sent = fixed + (1 - mine) * 2 ** order[k] + f
            copy = remote(
                src.at[(sent, *spans(q))],
                recv.at[q, slot],
                send_sem.at[q, slot],
                recv_sem.at[q, slot],
                {"col": partner},
            )
            items.append((copy, src, kept, slot))
        return items

    for k in range(bits + 1):
        for q in range(len(streams)):
            if k > 0:
                for copy, src, kept, slot in stage(q, k - 1):
                    copy.wait()
                    total = src[(kept, *spans(q))] + recv[q, slot]
                    if k == bits:
                        out[spans(q)] = total
                    else:
                        acc[(kept, *spans(q))] = total
            if k < bits:
                for copy, _, _, _ in stage(q, k):
                    copy.start()


def scattered(part):
    n = lax.axis_size("col")
    bits = n.bit_length() - 1
    rows, width = part.shape[0] // n, part.shape[1]
    return pl.pallas_call(
        functools.partial(scatter_kernel, bits),
        out_shape=jax.ShapeDtypeStruct((rows, width), jnp.float32),
        in_specs=[pl.BlockSpec(memory_space=pltpu.VMEM)],
        out_specs=pl.BlockSpec(memory_space=pltpu.VMEM),
        scratch_shapes=[
            pltpu.VMEM((n, rows, width), jnp.float32),
            pltpu.VMEM((4, n - 1, rows // 2, width // 2), jnp.float32),
            pltpu.SemaphoreType.DMA((4, n - 1)),
            pltpu.SemaphoreType.DMA((4, n - 1)),
        ],
        compiler_params=pltpu.CompilerParams(
            collective_id=1, has_side_effects=True, vmem_limit_bytes=VMEM_BYTES
        ),
        name="scatter",
    )(part.reshape(n, rows, width))


def core_kernel(row_bits, col_bits, part, out, acc, recv, send_sem, recv_sem):
    rows_axis = [("row", bit) for bit in range(row_bits)]
    cols_axis = [("col", bit) for bit in range(col_bits)]
    swap = {"grp": 1 - lax.axis_index("grp")}
    greet([{axis: peer(axis, bit)[1]} for axis, bit in rows_axis + cols_axis] + [swap])
    width = part.shape[0]
    half = width // 2
    orders = [
        cols_axis + rows_axis,
        cols_axis[::-1] + rows_axis,
        cols_axis + rows_axis,
        cols_axis[::-1] + rows_axis,
    ]
    lag = [0, 0, 2, 2]
    depth = row_bits + col_bits
    phases = 2 * depth + 1
    offsets = []
    for q, order in enumerate(orders):
        track = [(q // 2) * half]
        for k, (axis, bit) in enumerate(order):
            track.append(track[-1] + peer(axis, bit)[0] * (half >> (k + 1)))
        offsets.append(track)

    def describe(q, p):
        columns = pl.ds((q % 2) * half, half)
        sems = (send_sem.at[q, p], recv_sem.at[q, p])
        if p < depth:
            axis, bit = orders[q][p]
            mine, partner = peer(axis, bit)
            size = half >> (p + 1)
            sent = rows_at(offsets[q][p] + (1 - mine) * size, size)
            src = part if p == 0 else acc
            slot = pl.ds(half - (half >> p), size)
            return remote(src.at[sent, columns], recv.at[q, slot], *sems, {axis: partner})
        if p == depth:
            rows = rows_at(offsets[q][depth], half >> depth)
            return remote(acc.at[rows, columns], out.at[rows, columns], *sems, swap)
        level = 2 * depth + 1 - p
        axis, bit = orders[q][level - 1]
        rows = rows_at(offsets[q][level], half >> level)
        return remote(
            out.at[rows, columns], out.at[rows, columns], *sems, {axis: peer(axis, bit)[1]}
        )

    def finish(q, p):
        describe(q, p).wait()
        if p < depth:
            columns = pl.ds((q % 2) * half, half)
            size = half >> (p + 1)
            kept = rows_at(offsets[q][p + 1], size)
            src = part if p == 0 else acc
            acc[kept, columns] = src[kept, columns] + recv[q, pl.ds(half - (half >> p), size)]

    for tick in range(phases + 1 + max(lag)):
        for q in range(len(orders)):
            p = tick - lag[q]
            if 0 < p <= phases:
                finish(q, p - 1)
            if 0 <= p < phases:
                describe(q, p).start()


def other_core_of(part):
    width = part.shape[0]
    row_bits = lax.axis_size("row").bit_length() - 1
    col_bits = lax.axis_size("col").bit_length() - 1
    phases = 2 * (row_bits + col_bits) + 1
    return pl.pallas_call(
        functools.partial(core_kernel, row_bits, col_bits),
        out_shape=jax.ShapeDtypeStruct((width, width), jnp.float32),
        in_specs=[pl.BlockSpec(memory_space=pltpu.VMEM)],
        out_specs=pl.BlockSpec(memory_space=pltpu.VMEM),
        scratch_shapes=[
            pltpu.VMEM((width, width), jnp.float32),
            pltpu.VMEM((4, width // 2, width // 2), jnp.float32),
            pltpu.SemaphoreType.DMA((4, phases)),
            pltpu.SemaphoreType.DMA((4, phases)),
        ],
        compiler_params=pltpu.CompilerParams(
            collective_id=2, has_side_effects=True, vmem_limit_bytes=VMEM_BYTES
        ),
        name="core",
    )(part)


def shards(cost_matrix, coupling_factors):
    cost_tile = cost_matrix[0]
    current = coupling_factors[0]
    blk_rows = cost_tile.shape[0]
    rank_width = current.shape[1]
    for iteration in range(STEPS):
        panel_rows = gathered(current).reshape(blk_rows, rank_width)
        mixed = scattered(
            jnp.dot(
                cost_tile,
                panel_rows,
                precision=lax.Precision.HIGH,
                preferred_element_type=jnp.float32,
            )
        )
        core_part = lax.dot_general(
            current,
            mixed,
            (((0,), (0,)), ((), ())),
            precision=lax.Precision.HIGH,
            preferred_element_type=jnp.float32,
        )
        other_core = other_core_of(core_part)
        gradient = jnp.dot(
            mixed, other_core, precision=lax.Precision.HIGH, preferred_element_type=jnp.float32
        )
        row_scale = jnp.max(jnp.abs(gradient), axis=1, keepdims=True) + 1e-06
        exponent = -3.0 * gradient / row_scale
        weighted = current * jnp.exp(exponent)
        current = rank_width * weighted / jnp.sum(weighted, axis=1, keepdims=True)
    return current[None]


def solution(mesh):
    in_specs = (P("grp", "row", "col"), P("grp", ("row", "col"), None))
    out_specs = P("grp", ("row", "col"), None)
    return jax.shard_map(shards, mesh=mesh, in_specs=in_specs, out_specs=out_specs, check_vma=False)
```
